32 devices in a mesh: groups: 2 (over x), dom: 8 (over z, y), slab: 2 (over core).
Axes of the slice: x: 2, y: 2, z: 4, core: 2. Of those that a mesh axis runs over, the one named last changes fastest.
Arguments:
- features: bfloat16 [2, 2048, 512], P('slab', ('groups', 'dom')), parts along dimension 1, may hold values from -6 to 6
- orbitals: int32 [2, 2048], P('slab', ('groups', 'dom')), parts along dimension 1, may hold values from 4 to 13
- pair_list: int32 [2, 32768, 2], P('slab', ('groups', 'dom')), parts along dimension 1, may hold values from 0 to 671, as said below
- owners: int32 [2, 32768, 1], P('slab', ('groups', 'dom')), parts along dimension 1, may hold values from 0 to 7; in each aligned block of 2048 rows (0 to 2047, 2048 to 4095, ..., all dimensions but the last counted through in order) at most 384 rows name the same one
- edge_feats: bfloat16 [2, 32768, 128], P('slab', ('groups', 'dom')), parts along dimension 1, may hold values from -6 to 6
- cotangent: bfloat16 [2, 49152, 169], P('slab', ('groups', 'dom')), parts along dimension 1, may hold values from -6 to 6
- w_pair: bfloat16 [512, 512], replicated, may hold values from -0.25 to 0.25
- w_edge: bfloat16 [128, 512], replicated, may hold values from -0.5 to 0.5
- w_block: bfloat16 [512, 169], replicated, may hold values from -0.25 to 0.25
Outputs:
- block_out: bfloat16 [2, 49152, 169], P('slab', ('groups', 'dom')), parts along dimension 1
- atom_grads: float32 [2, 2048, 512], P('slab', ('groups', 'dom')), parts along dimension 1
- grad_pair: float32 [1024, 512], P('groups'), parts along dimension 0
- grad_edge: float32 [256, 512], P('groups'), parts along dimension 0
- grad_block: float32 [1024, 169], P('groups'), parts along dimension 0
The draws below stay inside these ranges and needn't reach their ends.
There are 2 independent parts, one for each index of `groups`. The reference program is written for one: setup_inputs(seed, part) draws one part's arguments, and reference() takes and returns one part's arrays. A program takes and returns all parts, laid end to end along the dimension named above; an argument that names none is the same for every part. Nothing has to cross between parts.
Inputs may be any that keep to these rules, and one draw needn't show every extreme that they name: pair_list[s, q, 0] lies in 0 to 127 and is 0 for the first task of each domain. With r = pair_list[s, q, 1] % 384: r lies in 96 to 287, and pair_list[s, q, 1] is below 768; the first task of each domain has the largest such value. `owners`: among the 2048 tasks of one domain, at most 384 have the same owner.
All inputs are finite; a program needn't handle non-finite values.
Results may differ from the reference program's by a relative error of at most 0.0056.
Values may be sent and summed in bfloat16 or wider, within the bound.
A program may use at most 64 MiB of HBM per device.

```python
import math
import jax
import jax.numpy as jnp
import numpy as np
from jax import lax

FEAT = 512
EDGE = 128
ORB = 13
BLOCK = 169
ATOM_DEV = 128
PAIR_DEV = 2048
RIM = 32
CAP = 384
NA = 1024
PAIRS_L = 16384
SLOTS = 24576
N_DOM = 8
N_SLAB = 2


def draw_pair_list(key, part):
    key = jax.random.fold_in(key, 7)
    key_own, key_kind, key_inner, key_rim = jax.random.split(key, 4)
    shape = (N_SLAB, PAIRS_L)
    own = jax.random.randint(key_own, shape, 0, ATOM_DEV)
    kind = jax.random.randint(key_kind, shape, 0, 8)
    inner = jax.random.randint(key_inner, shape, 0, ATOM_DEV)
    rim_pick = jax.random.randint(key_rim, shape, 0, RIM)
    offset = jnp.where(kind >= 4, 3 * ATOM_DEV, 0)
    sort_kind = kind % 4
    local = jnp.where(sort_kind < 2, ATOM_DEV + inner, jnp.where(sort_kind == 2, ATOM_DEV - RIM + rim_pick, 2 * ATOM_DEV + rim_pick))
    near = offset + local
    position = jnp.arange(PAIRS_L) % PAIR_DEV
    first = (position == 0)[None, :]
    near = jnp.where(first, 5 * ATOM_DEV + RIM - 1, near)
    own = jnp.where(first, 0, own)
    return jnp.stack([own, near], axis=-1).astype(jnp.int32)


def place_ends(values, rng, smallest, largest):
    extent = values.shape
    spot = [jax.random.randint(jax.random.fold_in(rng, axis), (), 0, extent[axis]) for axis in range(len(extent))]
    values = values.at[tuple(spot)].set(smallest)
    longest = extent.index(max(extent))
    spot[longest] = (spot[longest] + 1) % extent[longest]
    return values.at[tuple(spot)].set(largest)


def levels(rng, dims, cuts, smallest, top_value):
    def one(dim, shards_of):
        steps = jax.random.uniform(jax.random.fold_in(jax.random.fold_in(rng, 6), dim), (shards_of,), jnp.float32, smallest / len(cuts), top_value / len(cuts))
        return jnp.repeat(jnp.exp(steps), dims[dim] // shards_of).reshape((-1,) + (1,) * (len(dims) - dim - 1))

    factor_of = one(*cuts[0])
    for cut in cuts[1:]:
        factor_of = factor_of * one(*cut)
    return factor_of


def assign_block(key, own, number, rows, number_of, top, limit, lean):
    order = jax.random.permutation(key, number_of)
    heavy_load, ordinary = portions_of(number_of, rows * top, limit, lean, True), portions_of(number_of, rows * top, limit, lean, False)
    places = jnp.arange(number_of)

    def named(lengths, offset_by):
        used = int((lengths > 0).sum())
        fixed = max(1, used // 4)
        shifted = fixed + (places - fixed + offset_by * (used - fixed)) % max(1, number_of - fixed)
        return jnp.zeros((number_of,), jnp.int32).at[order[jnp.where(places < fixed, places, shifted)]].set(jnp.asarray(lengths, jnp.int32))

    lengths = jnp.where(number % 4 == 0, named(heavy_load, number // 4), named(ordinary, number - number // 4 - 1))
    mixed = jax.random.permutation(jax.random.fold_in(own, 3), number_of)
    source_of, receiver = mixed[0:number_of // 2 * 2:2], mixed[1:number_of // 2 * 2:2]
    room = jnp.minimum(lengths[source_of] - 1, limit - lengths[receiver]) // 2
    room = jnp.where((source_of == order[0]) | (receiver == order[0]) | (lengths[receiver] == 0), 0, jnp.maximum(room, 0))
    shifted = jax.random.randint(jax.random.fold_in(own, 4), (number_of // 2,), 0, 1 << 20) % (room + 1)
    lengths = lengths.at[source_of].add(-shifted).at[receiver].add(shifted)
    items = jnp.searchsorted(jnp.cumsum(lengths), jnp.arange(rows * top), side="right").astype(jnp.int32)
    listing = items.reshape(top, rows).T
    listing = listing[jax.random.permutation(jax.random.fold_in(own, 1), rows)]
    offset_by = jax.random.randint(jax.random.fold_in(own, 2), (rows, 1), 0, top)
    return jnp.take_along_axis(listing, (jnp.arange(top)[None, :] + offset_by) % top, axis=1)


def portions_of(number_of, total, reach, lean, full):
    loads = [(1 << 20) // math.isqrt(grade ** lean) + 1 for grade in range(1, number_of + 1)]
    largest = reach if full else min(reach, max(-(-total // number_of), total * loads[0] // sum(loads)))
    least = 1 if total - largest >= number_of - 1 else 0
    holding, spare = [largest] + [least] * (number_of - 1), total - largest - least * (number_of - 1)
    while spare > 0:
        free = [i for i in range(1, number_of) if holding[i] < largest] or [i for i in range(1, number_of) if holding[i] < reach]
        mass, budget = sum([loads[i] for i in free]), spare
        for i in free:
            extra = min(reach - holding[i], max(1, budget * loads[i] // mass), spare)
            holding[i] = holding[i] + extra
            spare = spare - extra
    return np.array(holding)


def bell_draw(key, dims, width, most, cuts=(), held_as=jnp.bfloat16):
    gain = levels(key, dims, cuts, -0.22, 0.18) if cuts else 1.0
    drawn = jax.random.normal(key, dims, jnp.float32) * width * gain
    return jnp.minimum(jnp.maximum(drawn, -most), most).astype(held_as)


def setup_inputs(seed: int = 0, part: int = 0) -> dict:
    key_of = jax.random.split(jax.random.key(seed), 10)
    part_keys = jax.random.split(jax.random.fold_in(key_of[9], part), 10)
    features = bell_draw(part_keys[0], (N_SLAB, NA, FEAT), 1.0, 6.0, ((0, 2), (1, 8)))
    orbitals = place_ends(jax.random.randint(part_keys[1], (N_SLAB, NA), 4, 14), jax.random.fold_in(part_keys[1], 1), 4, 13).astype(jnp.int32)
    pair_list = draw_pair_list(jax.random.fold_in(jax.random.fold_in(key_of[9], part), 71), part)
    owners_keys = jax.random.split(jax.random.fold_in(part_keys[3], 1), N_SLAB * PAIRS_L // PAIR_DEV)
    owners_turns = jax.random.permutation(jax.random.fold_in(part_keys[3], 3), N_SLAB * PAIRS_L // PAIR_DEV)
    owners = jax.vmap(lambda own, number: assign_block(jax.random.fold_in(part_keys[3], 2), own, number, PAIR_DEV, N_DOM, 1, CAP, 2))(owners_keys, owners_turns).reshape((N_SLAB, PAIRS_L, 1))
    edge_feats = bell_draw(part_keys[4], (N_SLAB, PAIRS_L, EDGE), 1.0, 6.0, ((0, 2), (1, 8)))
    cotangent = bell_draw(part_keys[5], (N_SLAB, SLOTS, BLOCK), 1.0, 6.0, ((0, 2), (1, 8)))
    w_pair = bell_draw(key_of[6], (FEAT, FEAT), FEAT ** -0.5, 0.25)
    w_edge = bell_draw(key_of[7], (EDGE, FEAT), EDGE ** -0.5, 0.5)
    w_block = bell_draw(key_of[8], (FEAT, BLOCK), FEAT ** -0.5, 0.25)
    return {"features": features, "orbitals": orbitals, "pair_list": pair_list, "owners": owners, "edge_feats": edge_feats, "cotangent": cotangent, "w_pair": w_pair, "w_edge": w_edge, "w_block": w_block}


def reference(features, orbitals, pair_list, owners, edge_feats, cotangent, w_pair, w_edge, w_block):
    entry = jnp.arange(BLOCK, dtype=jnp.int32)
    row_orb = entry // ORB
    col_orb = entry % ORB
    scale = float(N_SLAB * N_DOM * PAIR_DEV) ** -0.5
    doms = jnp.arange(N_DOM, dtype=jnp.int32)

    def step(carry, index):
        block_all, grads, gsum_pair, gsum_edge, gsum_block = carry
        layer = index // N_DOM
        domain = index % N_DOM
        start = (domain * PAIR_DEV).astype(jnp.int32)
        pairs = lax.dynamic_slice_in_dim(pair_list[layer], start, PAIR_DEV, 0)
        owner = lax.dynamic_slice_in_dim(owners[layer], start, PAIR_DEV, 0)[:, 0]
        edges = lax.dynamic_slice_in_dim(edge_feats[layer], start, PAIR_DEV, 0)
        own_atom = domain * ATOM_DEV + pairs[:, 0]
        jvals = pairs[:, 1]
        other = jnp.where(jvals >= 3 * ATOM_DEV, 1 - layer, layer)
        rest = jvals % (3 * ATOM_DEV)
        near = ((domain + rest // ATOM_DEV - 1) % N_DOM) * ATOM_DEV + rest % ATOM_DEV
        near = near.astype(jnp.int32)
        x_own = features[layer][own_atom]
        x_near = features[other, near]
        n_own = orbitals[layer][own_atom]
        n_near = orbitals[other, near]
        prod = (x_own.astype(jnp.float32) * x_near.astype(jnp.float32)).astype(jnp.bfloat16)
        pre = jnp.dot(prod, w_pair, preferred_element_type=jnp.float32) + jnp.dot(edges, w_edge, preferred_element_type=jnp.float32)
        act = jax.nn.silu(pre).astype(jnp.bfloat16)
        mask = (row_orb[None, :] < n_own[:, None]) & (col_orb[None, :] < n_near[:, None])
        raw = jnp.dot(act, w_block, preferred_element_type=jnp.float32)
        blocks = jnp.where(mask, raw, 0.0).astype(jnp.bfloat16)
        onehot = (owner[:, None] == doms[None, :]).astype(jnp.int32)
        rank = jnp.cumsum(onehot, axis=0)
        slot = jnp.sum(onehot * rank, axis=1) - 1
        rows = (owner * (N_DOM * CAP) + domain * CAP + slot).astype(jnp.int32)
        block_all = block_all.at[layer, rows].set(blocks)
        cot = cotangent[layer][rows]
        dblock = jnp.where(mask, cot, jnp.zeros_like(cot)).astype(jnp.bfloat16)
        dact = jnp.dot(dblock, w_block.T, preferred_element_type=jnp.float32)
        sg = jax.nn.sigmoid(pre)
        dpre = (dact * sg * (1.0 + pre * (1.0 - sg))).astype(jnp.bfloat16)
        dprod = jnp.dot(dpre, w_pair.T, preferred_element_type=jnp.float32)
        grads = grads.at[layer, own_atom].add(dprod * x_near.astype(jnp.float32))
        grads = grads.at[other, near].add(dprod * x_own.astype(jnp.float32))
        gsum_pair = gsum_pair + jnp.dot(prod.T, dpre, preferred_element_type=jnp.float32)
        gsum_edge = gsum_edge + jnp.dot(edges.T, dpre, preferred_element_type=jnp.float32)
        gsum_block = gsum_block + jnp.dot(act.T, dblock, preferred_element_type=jnp.float32)
        return (block_all, grads, gsum_pair, gsum_edge, gsum_block), None

    start_carry = (jnp.zeros((N_SLAB, SLOTS, BLOCK), jnp.bfloat16),
                   jnp.zeros((N_SLAB, NA, FEAT), jnp.float32),
                   jnp.zeros((FEAT, FEAT), jnp.float32),
                   jnp.zeros((EDGE, FEAT), jnp.float32),
                   jnp.zeros((FEAT, BLOCK), jnp.float32))
    final, unused = lax.scan(step, start_carry, jnp.arange(N_SLAB * N_DOM, dtype=jnp.int32))
    block_all, grads, gsum_pair, gsum_edge, gsum_block = final
    return (block_all, grads, gsum_pair * scale, gsum_edge * scale, gsum_block * scale)
```

```python
import functools

import jax
import jax.numpy as jnp
from jax import lax
from jax.experimental import pallas as pl
from jax.experimental.pallas import tpu as pltpu
from jax.sharding import PartitionSpec as P

ORB = 13
RIM = 32
LANE = 128
TILE = 256
F32 = jnp.float32
BF16 = jnp.bfloat16


def nn(a, b):
    return jnp.dot(a, b, preferred_element_type=F32)


def nt(a, b):
    return lax.dot_general(a, b, (((1,), (1,)), ((), ())), preferred_element_type=F32)


def tn(a, b):
    return lax.dot_general(a, b, (((0,), (0,)), ((), ())), preferred_element_type=F32)


def bits(cond):
    return jnp.where(cond, 1.0, 0.0).astype(BF16)


def iota(shape, dim):
    return lax.broadcasted_iota(jnp.int32, shape, dim)


def orbital_of(lanes):
    row = jnp.zeros_like(lanes)
    for k in range(1, 20):
        row = row + jnp.where(lanes >= ORB * k, 1, 0)
    return row.astype(F32), (lanes - ORB * row).astype(F32)


def kernel(
    D, C, T, A, FEAT, EDGE, BLOCK, PIECE, scale,
    feat_ref, orb_ref, pc_ref, oc_ref, rows_ref, edge_ref, cot_ref, wp_ref, we_ref, wb_ref,
    bo_ref, ag_ref, gp_ref, ge_ref, gb_ref,
    tab, wbp, cs, cr, bs, br, tr, tc, xo_s, xn_s, prod_s, act_s, ds_s, mask_s, blk, dc, cu,
    gt, gtb, gr, grp, gba, g32, gas, gar, hs, rb, fin,
    halo_s, halo_r, cot_s, cot_r, blk_s, blk_r, grad_s, grad_r, sum_s, sum_r, red_s, red_r,
    all_s, all_r, fwd_s, fwd_r,
):
    W = A + 2 * RIM
    C3 = C // 3
    S = D * C
    R = D * PIECE
    TAIL = BLOCK - LANE
    me = lax.axis_index("dom")
    slab = lax.axis_index("slab")
    other = 1 - slab
    nxt = lax.rem(me + 1, D)
    prv = lax.rem(me + D - 1, D)
    ntile = T // TILE

    def rcopy(src, dst, ssem, rsem, dom, layer):
        return pltpu.make_async_remote_copy(
            src_ref=src, dst_ref=dst, send_sem=ssem, recv_sem=rsem,
            device_id={"dom": dom, "slab": layer}, device_id_type=pl.DeviceIdType.MESH,
        )

    def peer(k):
        return lax.rem(me + k, D)

    def rows_at(t):
        return pl.ds(pl.multiple_of(t * TILE, TILE), TILE)

    barrier = pltpu.get_barrier_semaphore()

    @pl.loop(1, D)
    def _(k):
        pl.semaphore_signal(barrier, inc=1, device_id={"dom": peer(k), "slab": slab}, device_id_type=pl.DeviceIdType.MESH)

    for dom in (me, nxt, prv):
        pl.semaphore_signal(barrier, inc=1, device_id={"dom": dom, "slab": other}, device_id_type=pl.DeviceIdType.MESH)

    diag = jnp.where(iota((A, A), 0) == iota((A, A), 1), orb_ref[...].astype(F32), 0.0).astype(BF16)
    tab[RIM:RIM + A, 0:FEAT] = feat_ref[...]
    tab[RIM:RIM + A, FEAT:FEAT + LANE] = nn(diag, jnp.ones((A, LANE), BF16)).astype(BF16)
    pl.semaphore_wait(barrier, D + 2)

    head = tab.at[RIM:2 * RIM]
    tail = tab.at[A:A + RIM]
    halos = [
        rcopy(tail, tab.at[0:RIM], halo_s.at[0], halo_r.at[0], nxt, slab),
        rcopy(head, tab.at[RIM + A:W], halo_s.at[1], halo_r.at[1], prv, slab),
        rcopy(tail, tab.at[W:W + RIM], halo_s.at[2], halo_r.at[2], nxt, other),
        rcopy(head, tab.at[W + RIM + A:2 * W], halo_s.at[3], halo_r.at[3], prv, other),
        rcopy(tab.at[RIM:RIM + A], tab.at[W + RIM:W + RIM + A], halo_s.at[4], halo_r.at[4], me, other),
    ]
    for h in halos:
        h.start()

    def spread(g, height):
        return bits(iota((height, LANE), 0) + TAIL * g == iota((height, LANE), 1))

    def pack_cot(d, dst):
        base = pl.multiple_of(d * C, C)
        dst[d, 0:C, :] = cot_ref[pl.ds(base, C), 0:LANE]
        acc = None
        for g in range(3):
            part = nn(cot_ref[pl.ds(pl.multiple_of(base + g * C3, 16), C3), LANE:BLOCK], spread(g, TAIL))
            acc = part if acc is None else acc + part
        dst[d, C:C + C3, :] = acc.astype(BF16)

    def exchange(src, dst, ssem, rsem, d, at):
        return rcopy(src.at[d], dst.at[at], ssem.at[d], rsem.at[at], d, slab)

    @pl.loop(1, D)
    def _(k):
        d = peer(k)
        pack_cot(d, cs)
        exchange(cs, cr, cot_s, cot_r, d, me).start()

    pack_cot(me, cr)

    wbp[...] = jnp.zeros_like(wbp)
    wbp[:, 0:LANE] = wb_ref[:, 0:LANE]
    wbp[:, LANE:BLOCK] = wb_ref[:, LANE:BLOCK]

    DP = max(16, D)
    upper = bits(iota((TILE, TILE), 0) <= iota((TILE, TILE), 1))
    lower = bits(iota((TILE, TILE), 0) >= iota((TILE, TILE), 1))

    def slots(t, carry):
        down, across = carry
        at = rows_at(t)
        ow = rows_ref[2:3, at]
        hit = jnp.where(iota((DP, TILE), 0) == ow, 1.0, 0.0)
        rank = nn(hit.astype(BF16), upper) + down
        slot = jnp.sum(hit * rank, axis=0, keepdims=True) - 1.0
        tr[0:1, at] = ow * C + slot.astype(jnp.int32)
        oc = oc_ref[at, 0:1]
        hit_c = jnp.where(iota((TILE, LANE), 1) == oc, 1.0, 0.0)
        rank_c = nn(lower, hit_c.astype(BF16)) + across
        slot_c = jnp.sum(hit_c * rank_c, axis=1, keepdims=True) - 1.0
        tc[at, 0:1] = oc * C + slot_c.astype(jnp.int32)
        return down + jnp.sum(hit, axis=1, keepdims=True), across + jnp.sum(hit_c, axis=0, keepdims=True)

    lax.fori_loop(0, ntile, slots, (jnp.zeros((DP, 1), F32), jnp.zeros((1, LANE), F32)))

    for h in halos:
        h.wait_recv()

    def table_row(raw):
        return jnp.where(raw >= 3 * A, raw - 3 * A + W, raw) - (A - RIM)

    lane = iota((1, LANE), 1)
    div_hi, mod_hi = orbital_of(lane)
    div_lo, mod_lo = orbital_of(lane + LANE)

    @pl.loop(0, ntile)
    def _(t):
        at = rows_at(t)
        oh_own = bits(iota((TILE, A), 1) == pc_ref[at, 0:1])
        oh_near = bits(iota((TILE, 2 * W), 1) == table_row(pc_ref[at, 1:2]))
        xo = nn(oh_own, tab[RIM:RIM + A, :])
        xn = nn(oh_near, tab[...])
        xo_s[at, :] = xo[:, 0:FEAT].astype(BF16)
        xn_s[at, :] = xn[:, 0:FEAT].astype(BF16)
        prod = (xo[:, 0:FEAT] * xn[:, 0:FEAT]).astype(BF16)
        prod_s[at, :] = prod
        pre = nn(prod, wp_ref[...]) + nn(edge_ref[at, :], we_ref[...])
        sg = jax.nn.sigmoid(pre)
        act = (pre * sg).astype(BF16)
        act_s[at, :] = act
        ds_s[at, :] = sg * (1.0 + pre * (1.0 - sg))
        raw = nn(act, wbp[...])
        no, near = xo[:, FEAT:FEAT + LANE], xn[:, FEAT:FEAT + LANE]
        for i, (div, mod) in enumerate(((div_hi, mod_hi), (div_lo, mod_lo))):
            keep = (div < no) & (mod < near)
            mask_s[at, i * LANE:(i + 1) * LANE] = bits(keep)
            blk[at, i * LANE:(i + 1) * LANE] = jnp.where(keep, raw[:, i * LANE:(i + 1) * LANE], 0.0).astype(BF16)

    def pack_blocks(d, dst):
        acc = jnp.zeros((C, 2 * LANE), F32)
        step = 2 * TILE
        for j in range(T // step):
            hit = bits(iota((C, step), 0) + d * C == tr[0:1, j * step:(j + 1) * step])
            acc = acc + nn(hit, blk[j * step:(j + 1) * step, :])
        dst[d, 0:C, :] = acc[:, 0:LANE].astype(BF16)
        low = acc[:, LANE:2 * LANE].astype(BF16)
        packed = None
        for g in range(3):
            part = nn(low[g * C3:(g + 1) * C3, :], spread(g, LANE))
            packed = part if packed is None else packed + part
        dst[d, C:C + C3, :] = packed.astype(BF16)

    @pl.loop(1, D)
    def _(k):
        d = peer(k)
        pack_blocks(d, bs)
        exchange(bs, br, blk_s, blk_r, d, me).start()

    pack_blocks(me, br)

    def pick(g):
        row, col = iota((LANE, LANE), 0), iota((LANE, LANE), 1)
        return bits((row == col + TAIL * g) & (col < TAIL))

    dc[...] = jnp.zeros_like(dc)

    def collect(d):
        cu[:, 0:LANE] = cr[d, 0:C, :]
        packed = cr[d, C:C + C3, :]
        for g in range(3):
            cu[g * C3:(g + 1) * C3, LANE:2 * LANE] = nn(packed, pick(g)).astype(BF16)
        for t in range(ntile):
            at = slice(t * TILE, (t + 1) * TILE)
            hit = bits(iota((TILE, C), 1) + d * C == tc[at, 0:1])
            dc[at, :] += nn(hit, cu[...])

    collect(me)

    @pl.loop(1, D)
    def _(k):
        d = lax.rem(me + D - k, D)
        exchange(cs, cr, cot_s, cot_r, d, d).wait_recv()
        collect(d)

    gt[...] = jnp.zeros_like(gt)
    gp_ref[...] = jnp.zeros_like(gp_ref)
    ge_ref[...] = jnp.zeros_like(ge_ref)
    gba[...] = jnp.zeros_like(gba)

    @pl.loop(0, ntile)
    def _(t):
        at = rows_at(t)
        dblock = (dc[at, :] * mask_s[at, :].astype(F32)).astype(BF16)
        dact = nt(dblock, wbp[...])
        dpre = (dact * ds_s[at, :]).astype(BF16)
        gp_ref[...] += tn(prod_s[at, :], dpre)
        ge_ref[...] += tn(edge_ref[at, :], dpre)
        gba[...] += tn(act_s[at, :], dblock)
        dprod = nt(dpre, wp_ref[...])
        to_own = (dprod * xn_s[at, :].astype(F32)).astype(BF16)
        to_near = (dprod * xo_s[at, :].astype(F32)).astype(BF16)
        near_hit = bits(iota((2 * W, TILE), 0) == table_row(rows_ref[1:2, at]))
        own_hit = bits(iota((A, TILE), 0) == rows_ref[0:1, at])
        gt[...] += nn(near_hit, to_near)
        gt[RIM:RIM + A, :] += nn(own_hit, to_own)

    if 2 * R > 4 * FEAT + 4 * EDGE + 2 * FEAT:
        g32[...] = jnp.zeros_like(g32)
    for c in range(4):
        g32[c * FEAT:(c + 1) * FEAT, :] = gp_ref[:, c * LANE:(c + 1) * LANE]
        g32[4 * FEAT + c * EDGE:4 * FEAT + (c + 1) * EDGE, :] = ge_ref[:, c * LANE:(c + 1) * LANE]
    low = 4 * FEAT + 4 * EDGE
    for c in range(2):
        g32[low + c * FEAT:low + (c + 1) * FEAT, :] = gba[:, c * LANE:(c + 1) * LANE]
    gas[...] = g32[pl.ds(pl.multiple_of(other * R, 16), R), :].astype(BF16)
    swap = rcopy(gas, gar, sum_s, sum_r, me, other)
    swap.start()

    gtb[...] = gt[...].astype(BF16)
    grads = [
        rcopy(gtb.at[0:RIM], gr.at[0], grad_s.at[0], grad_r.at[0], prv, slab),
        rcopy(gtb.at[RIM + A:W], gr.at[1], grad_s.at[1], grad_r.at[1], nxt, slab),
        rcopy(gtb.at[W:W + RIM], gr.at[2], grad_s.at[2], grad_r.at[2], prv, other),
        rcopy(gtb.at[W + RIM + A:2 * W], gr.at[3], grad_s.at[3], grad_r.at[3], nxt, other),
        rcopy(gtb.at[W + RIM:W + RIM + A], grp, grad_s.at[4], grad_r.at[4], me, other),
    ]
    for g in grads:
        g.start()

    swap.wait_recv()
    hs[...] = (g32[pl.ds(pl.multiple_of(slab * R, 16), R), :] + gar[...].astype(F32)).astype(BF16)

    def piece(d, of=0):
        return pl.ds(pl.multiple_of(of * R + d * PIECE, 16), PIECE)

    def reduce_copy(d, at):
        return rcopy(hs.at[piece(d)], rb.at[at], red_s.at[d], red_r.at[at], d, slab)

    @pl.loop(1, D)
    def _(k):
        reduce_copy(peer(k), me).start()

    for g in grads:
        g.wait_recv()
    ag_ref[...] = gt[RIM:RIM + A, :] + grp[...].astype(F32)
    ag_ref[A - RIM:A, :] += gr[0].astype(F32) + gr[2].astype(F32)
    ag_ref[0:RIM, :] += gr[1].astype(F32) + gr[3].astype(F32)

    def add_up(k, total):
        s = lax.rem(me + D - k, D)
        reduce_copy(s, s).wait_recv()
        return total + rb[s].astype(F32)

    total = lax.fori_loop(1, D, add_up, g32[piece(me, slab), :] + gar[piece(me), :].astype(F32))
    fin[piece(me, slab), :] = total.astype(BF16)

    def gather_copy(d, at):
        return rcopy(fin.at[piece(at, slab)], fin.at[piece(at, slab)], all_s.at[d], all_r.at[at], d, slab)

    def forward_copy(s, of):
        return rcopy(fin.at[piece(s, of)], fin.at[piece(s, of)], fwd_s.at[s], fwd_r.at[s], me, other)

    @pl.loop(1, D)
    def _(k):
        gather_copy(peer(k), me).start()

    forward_copy(me, slab).start()

    def unpack(d):
        base = d * C
        bo_ref[pl.ds(pl.multiple_of(base, 16), C), 0:LANE] = br[d, 0:C, :]
        packed = br[d, C:C + C3, :]
        for g in range(3):
            part = nn(packed, pick(g)).astype(BF16)
            bo_ref[pl.ds(pl.multiple_of(base + g * C3, 16), C3), LANE:BLOCK] = part[:, 0:TAIL]

    unpack(me)

    @pl.loop(1, D)
    def _(k):
        d = lax.rem(me + D - k, D)
        exchange(bs, br, blk_s, blk_r, d, d).wait_recv()
        unpack(d)

    @pl.loop(1, D)
    def _(k):
        s = lax.rem(me + D - k, D)
        gather_copy(s, s).wait_recv()
        forward_copy(s, slab).start()

    @pl.loop(0, D)
    def _(s):
        forward_copy(s, other).wait_recv()

    for c in range(4):
        gp_ref[:, c * LANE:(c + 1) * LANE] = fin[c * FEAT:(c + 1) * FEAT, :].astype(F32) * scale
        ge_ref[:, c * LANE:(c + 1) * LANE] = fin[4 * FEAT + c * EDGE:4 * FEAT + (c + 1) * EDGE, :].astype(F32) * scale
    gb_ref[:, 0:LANE] = fin[low:low + FEAT, :].astype(F32) * scale
    gb_ref[:, LANE:BLOCK] = fin[low + FEAT:low + 2 * FEAT, 0:TAIL].astype(F32) * scale

    for h in halos + grads + [swap]:
        h.wait_send()

    @pl.loop(1, D)
    def _(k):
        d = peer(k)
        exchange(cs, cr, cot_s, cot_r, d, me).wait_send()
        exchange(bs, br, blk_s, blk_r, d, me).wait_send()
        reduce_copy(d, me).wait_send()
        gather_copy(d, me).wait_send()

    @pl.loop(0, D)
    def _(s):
        forward_copy(s, slab).wait_send()


def shards(features, orbitals, pair_list, owners, edge_feats, cotangent, w_pair, w_edge, w_block):
    A, FEAT = features.shape[1:]
    T = pair_list.shape[1]
    D = lax.axis_size("dom")
    S, BLOCK = cotangent.shape[1:]
    EDGE = edge_feats.shape[2]
    C = S // D
    W = A + 2 * RIM
    flat = 4 * FEAT + 4 * EDGE + 2 * FEAT
    PIECE = -(-flat // (2 * D * 16)) * 16
    R = D * PIECE
    scale = float(lax.axis_size("slab") * D * T) ** (-0.5)
    rows = jnp.concatenate([pair_list[0], owners[0]], axis=1).T
    row_len = C + C // 3
    dma = pltpu.SemaphoreType.DMA
    vmem = pl.BlockSpec(memory_space=pltpu.VMEM)
    outs = pl.pallas_call(
        functools.partial(kernel, D, C, T, A, FEAT, EDGE, BLOCK, PIECE, scale),
        out_shape=(
            jax.ShapeDtypeStruct((S, BLOCK), BF16),
            jax.ShapeDtypeStruct((A, FEAT), F32),
            jax.ShapeDtypeStruct((FEAT, FEAT), F32),
            jax.ShapeDtypeStruct((EDGE, FEAT), F32),
            jax.ShapeDtypeStruct((FEAT, BLOCK), F32),
        ),
        in_specs=[vmem] * 10,
        out_specs=(vmem,) * 5,
        scratch_shapes=[
            pltpu.VMEM((2 * W, FEAT + LANE), BF16),
            pltpu.VMEM((FEAT, 2 * LANE), BF16),
            pltpu.VMEM((D, row_len, LANE), BF16),
            pltpu.VMEM((D, row_len, LANE), BF16),
            pltpu.VMEM((D, row_len, LANE), BF16),
            pltpu.VMEM((D, row_len, LANE), BF16),
            pltpu.VMEM((8, T), jnp.int32),
            pltpu.VMEM((T, 1), jnp.int32),
            pltpu.VMEM((T, FEAT), BF16),
            pltpu.VMEM((T, FEAT), BF16),
            pltpu.VMEM((T, FEAT), BF16),
            pltpu.VMEM((T, FEAT), BF16),
            pltpu.VMEM((T, FEAT), F32),
            pltpu.VMEM((T, 2 * LANE), BF16),
            pltpu.VMEM((T, 2 * LANE), BF16),
            pltpu.VMEM((T, 2 * LANE), F32),
            pltpu.VMEM((C, 2 * LANE), BF16),
            pltpu.VMEM((2 * W, FEAT), F32),
            pltpu.VMEM((2 * W, FEAT), BF16),
            pltpu.VMEM((4, RIM, FEAT), BF16),
            pltpu.VMEM((A, FEAT), BF16),
            pltpu.VMEM((FEAT, 2 * LANE), F32),
            pltpu.VMEM((2 * R, LANE), F32),
            pltpu.VMEM((R, LANE), BF16),
            pltpu.VMEM((R, LANE), BF16),
            pltpu.VMEM((R, LANE), BF16),
            pltpu.VMEM((D, PIECE, LANE), BF16),
            pltpu.VMEM((2 * R, LANE), BF16),
            dma((5,)), dma((5,)), dma((D,)), dma((D,)), dma((D,)), dma((D,)), dma((5,)), dma((5,)),
            dma, dma, dma((D,)), dma((D,)), dma((D,)), dma((D,)), dma((D,)), dma((D,)),
        ],
        compiler_params=pltpu.CompilerParams(
            collective_id=0, has_side_effects=True, vmem_limit_bytes=56 * 1024 * 1024
        ),
        cost_estimate=pl.CostEstimate(flops=15 * 10**9, bytes_accessed=10**7, transcendentals=T * FEAT),
    )(features[0], orbitals, pair_list[0], owners[0], rows, edge_feats[0], cotangent[0], w_pair, w_edge, w_block)
    return (outs[0][None], outs[1][None], *outs[2:])


def solution(mesh):
    spread = P("slab", ("groups", "dom"), None)
    in_specs = (spread, P("slab", ("groups", "dom")), spread, spread, spread, spread, P(), P(), P())
    out_specs = (spread, spread, P("groups", None), P("groups", None), P("groups", None))
    return jax.shard_map(shards, mesh=mesh, in_specs=in_specs, out_specs=out_specs, check_vma=False)
```

```python
import functools

import jax
import jax.numpy as jnp
from jax import lax
from jax.experimental import pallas as pl
from jax.experimental.pallas import tpu as pltpu
from jax.sharding import PartitionSpec as P

ORB = 13
RIM = 32
LANE = 128
TILE = 256
F32 = jnp.float32
BF16 = jnp.bfloat16


def nn(a, b):
    return jnp.dot(a, b, preferred_element_type=F32)


def nt(a, b):
    return lax.dot_general(a, b, (((1,), (1,)), ((), ())), preferred_element_type=F32)


def tn(a, b):
    return lax.dot_general(a, b, (((0,), (0,)), ((), ())), preferred_element_type=F32)


def bits(cond):
    return jnp.where(cond, 1.0, 0.0).astype(BF16)


def iota(shape, dim):
    return lax.broadcasted_iota(jnp.int32, shape, dim)


def orbital_of(lanes):
    row = jnp.zeros_like(lanes)
    for k in range(1, 20):
        row = row + jnp.where(lanes >= ORB * k, 1, 0)
    return row.astype(F32), (lanes - ORB * row).astype(F32)


def kernel(
    D, C, T, A, FEAT, EDGE, BLOCK, PIECE, scale,
    feat_ref, orb_ref, pair_ref, own_ref, edge_ref, cot_ref, wp_ref, we_ref, wb_ref,
    bo_ref, ag_ref, gp_ref, ge_ref, gb_ref,
    tab, wbp, cs, cr, bs, br, vr, vc, xo_s, xn_s, prod_s, act_s, ds_s, mask_s, blk, dc,
    gt, gtb, gr, grp, gba, g32, gas, gar, hs, rb, fin,
    halo_s, halo_r, cot_s, cot_r, blk_s, blk_r, grad_s, grad_r, sum_s, sum_r, red_s, red_r,
    all_s, all_r, fwd_s, fwd_r,
):
    W = A + 2 * RIM
    FULL = wbp.shape[0]
    CUT = FULL - 16
    R = D * PIECE
    me = lax.axis_index("dom")
    slab = lax.axis_index("slab")
    other = 1 - slab
    nxt = lax.rem(me + 1, D)
    prv = lax.rem(me + D - 1, D)
    ntile = T // TILE

    def rcopy(src, dst, ssem, rsem, dom, layer):
        return pltpu.make_async_remote_copy(
            src_ref=src, dst_ref=dst, send_sem=ssem, recv_sem=rsem,
            device_id={"dom": dom, "slab": layer}, device_id_type=pl.DeviceIdType.MESH,
        )

    def peer(k):
        i = k - 1
        return lax.rem(me + D // 2 + (1 - 2 * (i % 2)) * ((i + 1) // 2), D)

    def source(k):
        i = k - 1
        return lax.rem(me + 2 * D - D // 2 - (1 - 2 * (i % 2)) * ((i + 1) // 2), D)

    def rows_at(t):
        return pl.ds(pl.multiple_of(t * TILE, TILE), TILE)

    barrier = pltpu.get_barrier_semaphore()

    @pl.loop(1, D)
    def _(k):
        pl.semaphore_signal(barrier, inc=1, device_id={"dom": peer(k), "slab": slab}, device_id_type=pl.DeviceIdType.MESH)

    for dom in (me, nxt, prv):
        pl.semaphore_signal(barrier, inc=1, device_id={"dom": dom, "slab": other}, device_id_type=pl.DeviceIdType.MESH)

    diag = jnp.where(iota((A, A), 0) == iota((A, A), 1), orb_ref[...].astype(F32), 0.0).astype(BF16)
    tab[RIM:RIM + A, 0:FEAT] = feat_ref[...]
    tab[RIM:RIM + A, FEAT:FEAT + LANE] = nn(diag, jnp.ones((A, LANE), BF16)).astype(BF16)
    pl.semaphore_wait(barrier, D + 2)

    head = tab.at[RIM:2 * RIM]
    tail = tab.at[A:A + RIM]
    halos = [
        rcopy(tail, tab.at[0:RIM], halo_s.at[0], halo_r.at[0], nxt, slab),
        rcopy(head, tab.at[RIM + A:W], halo_s.at[1], halo_r.at[1], prv, slab),
        rcopy(tail, tab.at[W:W + RIM], halo_s.at[2], halo_r.at[2], nxt, other),
        rcopy(head, tab.at[W + RIM + A:2 * W], halo_s.at[3], halo_r.at[3], prv, other),
        rcopy(tab.at[RIM:RIM + A], tab.at[W + RIM:W + RIM + A], halo_s.at[4], halo_r.at[4], me, other),
    ]
    for h in halos:
        h.start()

    cs[:, CUT:FULL, :] = jnp.zeros((D, 16, C), BF16)
    cr[me, CUT:FULL, :] = jnp.zeros((16, C), BF16)

    def take_cot(d, dst):
        at = pl.ds(pl.multiple_of(d * C, C), C)
        dst[d, 0:CUT, :] = cot_ref[0:CUT, at]
        dst[d, CUT:BLOCK, :] = cot_ref[CUT:BLOCK, at]

    def exchange(src, dst, ssem, rsem, d, at):
        return rcopy(src.at[d], dst.at[at], ssem.at[d], rsem.at[at], d, slab)

    @pl.loop(1, D)
    def _(k):
        d = peer(k)
        take_cot(d, cs)
        exchange(cs, cr, cot_s, cot_r, d, me).start()

    take_cot(me, cr)

    wbp[CUT:FULL, :] = jnp.zeros((16, FEAT), BF16)
    wbp[0:CUT, :] = wb_ref[0:CUT, :]
    wbp[CUT:BLOCK, :] = wb_ref[CUT:BLOCK, :]

    def table_row(raw):
        return jnp.where(raw >= 3 * A, raw - 3 * A + W, raw) - (A - RIM)

    DP = max(16, D)
    upper = bits(iota((TILE, TILE), 0) <= iota((TILE, TILE), 1))
    down = jnp.zeros((DP, 1), F32)
    vr[0:1, :] = pair_ref[0:1, :].astype(F32)
    vr[1:2, :] = table_row(pair_ref[1:2, :]).astype(F32)
    vr[3:8, :] = jnp.zeros((5, T), F32)
    for t in range(ntile):
        at = slice(t * TILE, (t + 1) * TILE)
        ow = own_ref[0:1, at]
        hit = jnp.where(iota((DP, TILE), 0) == ow, 1.0, 0.0)
        rank = nn(hit.astype(BF16), upper) + down
        slot = jnp.sum(hit * rank, axis=0, keepdims=True) - 1.0
        vr[2:3, at] = (ow * C).astype(F32) + slot
        down = down + jnp.sum(hit, axis=1, keepdims=True)
        vc[at, :] = vr[:, at].T

    for h in halos:
        h.wait_recv()

    entry = iota((FULL, 1), 0)
    div, mod = orbital_of(entry)
    first = bits(iota((16, LANE), 1) == 0)
    count_all = nt(first, tab[:, FEAT:FEAT + LANE]).astype(BF16)
    count_own = nt(first, tab[RIM:RIM + A, FEAT:FEAT + LANE]).astype(BF16)
    lanes_own = iota((TILE, A), 1).astype(F32)
    lanes_near = iota((TILE, 2 * W), 1).astype(F32)

    def hits_row(at):
        own = bits(iota((A, TILE), 0).astype(F32) == vr[0:1, at])
        near = bits(iota((2 * W, TILE), 0).astype(F32) == vr[1:2, at])
        return own, near

    @pl.loop(0, ntile)
    def _(t):
        at = rows_at(t)
        own_hit, near_hit = hits_row(at)
        no = nn(count_own, own_hit)[0:1, :]
        near = nn(count_all, near_hit)[0:1, :]
        keep = (div < no) & (mod < near)
        mask_s[:, at] = bits(keep)
        xo = nn(bits(lanes_own == vc[at, 0:1]), tab[RIM:RIM + A, 0:FEAT])
        xn = nn(bits(lanes_near == vc[at, 1:2]), tab[:, 0:FEAT])
        xo_s[at, :] = xo.astype(BF16)
        xn_s[at, :] = xn.astype(BF16)
        prod = (xo * xn).astype(BF16)
        prod_s[at, :] = prod
        pre = nn(prod, wp_ref[...]) + nn(edge_ref[at, :], we_ref[...])
        sg = jax.nn.sigmoid(pre)
        act = (pre * sg).astype(BF16)
        act_s[at, :] = act
        ds_s[at, :] = sg * (1.0 + pre * (1.0 - sg))
        blk[:, at] = jnp.where(keep, nt(wbp[...], act), 0.0).astype(BF16)

    STEP = 2 * TILE

    def pack_blocks(d, dst):
        acc = jnp.zeros((FULL, C), F32)
        base = (d * C).astype(F32)
        slot_of = iota((STEP, C), 1).astype(F32)
        for j in range(T // STEP):
            at = slice(j * STEP, (j + 1) * STEP)
            acc = acc + nn(blk[:, at], bits(slot_of == vc[at, 2:3] - base))
        dst[d] = acc.astype(BF16)

    @pl.loop(1, D)
    def _(k):
        d = peer(k)
        pack_blocks(d, bs)
        exchange(bs, br, blk_s, blk_r, d, me).start()

    pack_blocks(me, br)

    dc[...] = jnp.zeros_like(dc)

    def collect(d):
        base = (d * C).astype(F32)
        slot_of = iota((C, STEP), 0).astype(F32)
        for j in range(T // STEP):
            at = slice(j * STEP, (j + 1) * STEP)
            dc[:, at] += nn(cr[d], bits(slot_of == vr[2:3, at] - base))

    collect(me)

    @pl.loop(1, D)
    def _(k):
        d = source(k)
        exchange(cs, cr, cot_s, cot_r, d, d).wait_recv()
        collect(d)

    gt[...] = jnp.zeros_like(gt)
    gp_ref[...] = jnp.zeros_like(gp_ref)
    ge_ref[...] = jnp.zeros_like(ge_ref)
    gba[...] = jnp.zeros_like(gba)

    @pl.loop(0, ntile)
    def _(t):
        at = rows_at(t)
        dblock = (dc[:, at] * mask_s[:, at].astype(F32)).astype(BF16)
        dact = tn(dblock, wbp[...])
        dpre = (dact * ds_s[at, :]).astype(BF16)
        gp_ref[...] += tn(prod_s[at, :], dpre)
        ge_ref[...] += tn(edge_ref[at, :], dpre)
        gba[...] += nn(dblock, act_s[at, :])
        dprod = nt(dpre, wp_ref[...])
        to_own = (dprod * xn_s[at, :].astype(F32)).astype(BF16)
        to_near = (dprod * xo_s[at, :].astype(F32)).astype(BF16)
        own_hit, near_hit = hits_row(at)
        gt[...] += nn(near_hit, to_near)
        gt[RIM:RIM + A, :] += nn(own_hit, to_own)

    if 2 * R > 4 * (FEAT + EDGE + FULL):
        g32[4 * (FEAT + EDGE + FULL):2 * R, :] = jnp.zeros((2 * R - 4 * (FEAT + EDGE + FULL), LANE), F32)
    for c in range(4):
        g32[c * FEAT:(c + 1) * FEAT, :] = gp_ref[:, c * LANE:(c + 1) * LANE]
        g32[4 * FEAT + c * EDGE:4 * FEAT + (c + 1) * EDGE, :] = ge_ref[:, c * LANE:(c + 1) * LANE]
    low = 4 * FEAT + 4 * EDGE
    for c in range(4):
        g32[low + c * FULL:low + (c + 1) * FULL, :] = gba[:, c * LANE:(c + 1) * LANE]
    gas[...] = g32[pl.ds(pl.multiple_of(other * R, 16), R), :].astype(BF16)
    swap = rcopy(gas, gar, sum_s, sum_r, me, other)
    swap.start()

    gtb[...] = gt[...].astype(BF16)
    grads = [
        rcopy(gtb.at[0:RIM], gr.at[0], grad_s.at[0], grad_r.at[0], prv, slab),
        rcopy(gtb.at[RIM + A:W], gr.at[1], grad_s.at[1], grad_r.at[1], nxt, slab),
        rcopy(gtb.at[W:W + RIM], gr.at[2], grad_s.at[2], grad_r.at[2], prv, other),
        rcopy(gtb.at[W + RIM + A:2 * W], gr.at[3], grad_s.at[3], grad_r.at[3], nxt, other),
        rcopy(gtb.at[W + RIM:W + RIM + A], grp, grad_s.at[4], grad_r.at[4], me, other),
    ]
    for g in grads:
        g.start()

    swap.wait_recv()
    hs[...] = (g32[pl.ds(pl.multiple_of(slab * R, 16), R), :] + gar[...].astype(F32)).astype(BF16)

    def piece(d, of=0):
        return pl.ds(pl.multiple_of(of * R + d * PIECE, 16), PIECE)

    def reduce_copy(d, at):
        return rcopy(hs.at[piece(d)], rb.at[at], red_s.at[d], red_r.at[at], d, slab)

    @pl.loop(1, D)
    def _(k):
        reduce_copy(peer(k), me).start()

    for g in grads:
        g.wait_recv()
    ag_ref[...] = gt[RIM:RIM + A, :] + grp[...].astype(F32)
    ag_ref[A - RIM:A, :] += gr[0].astype(F32) + gr[2].astype(F32)
    ag_ref[0:RIM, :] += gr[1].astype(F32) + gr[3].astype(F32)

    def add_up(k, total):
        s = source(k)
        reduce_copy(s, s).wait_recv()
        return total + rb[s].astype(F32)

    total = lax.fori_loop(1, D, add_up, g32[piece(me, slab), :] + gar[piece(me), :].astype(F32))
    fin[piece(me, slab), :] = total.astype(BF16)

    def gather_copy(d, at):
        return rcopy(fin.at[piece(at, slab)], fin.at[piece(at, slab)], all_s.at[d], all_r.at[at], d, slab)

    def forward_copy(s, of):
        return rcopy(fin.at[piece(s, of)], fin.at[piece(s, of)], fwd_s.at[s], fwd_r.at[s], me, other)

    @pl.loop(1, D)
    def _(k):
        gather_copy(peer(k), me).start()

    forward_copy(me, slab).start()

    def unpack(d):
        at = pl.ds(pl.multiple_of(d * C, C), C)
        bo_ref[0:CUT, at] = br[d, 0:CUT, :]
        bo_ref[CUT:BLOCK, at] = br[d, CUT:BLOCK, :]

    unpack(me)

    @pl.loop(1, D)
    def _(k):
        d = source(k)
        exchange(bs, br, blk_s, blk_r, d, d).wait_recv()
        unpack(d)

    @pl.loop(1, D)
    def _(k):
        s = source(k)
        gather_copy(s, s).wait_recv()
        forward_copy(s, slab).start()

    @pl.loop(0, D)
    def _(s):
        forward_copy(s, other).wait_recv()

    for c in range(4):
        gp_ref[:, c * LANE:(c + 1) * LANE] = fin[c * FEAT:(c + 1) * FEAT, :].astype(F32) * scale
        ge_ref[:, c * LANE:(c + 1) * LANE] = fin[4 * FEAT + c * EDGE:4 * FEAT + (c + 1) * EDGE, :].astype(F32) * scale
    for c in range(4):
        gb_ref[:, c * LANE:(c + 1) * LANE] = fin[low + c * FULL:low + c * FULL + BLOCK, :].astype(F32) * scale

    for h in halos + grads + [swap]:
        h.wait_send()

    @pl.loop(1, D)
    def _(k):
        d = peer(k)
        exchange(cs, cr, cot_s, cot_r, d, me).wait_send()
        exchange(bs, br, blk_s, blk_r, d, me).wait_send()
        reduce_copy(d, me).wait_send()
        gather_copy(d, me).wait_send()

    @pl.loop(0, D)
    def _(s):
        forward_copy(s, slab).wait_send()


def shards(features, orbitals, pair_list, owners, edge_feats, cotangent, w_pair, w_edge, w_block):
    A, FEAT = features.shape[1:]
    T = pair_list.shape[1]
    D = lax.axis_size("dom")
    S, BLOCK = cotangent.shape[1:]
    EDGE = edge_feats.shape[2]
    C = S // D
    CP = -(-C // LANE) * LANE
    W = A + 2 * RIM
    FULL = -(-BLOCK // 16) * 16
    flat = 4 * (FEAT + EDGE + FULL)
    PIECE = -(-flat // (2 * D * 16)) * 16
    R = D * PIECE
    scale = float(lax.axis_size("slab") * D * T) ** (-0.5)
    cot = cotangent[0].T
    if CP != C:
        cot = jnp.pad(cot.reshape(BLOCK, D, C), ((0, 0), (0, 0), (0, CP - C))).reshape(BLOCK, D * CP)
    dma = pltpu.SemaphoreType.DMA
    vmem = pl.BlockSpec(memory_space=pltpu.VMEM)
    outs = pl.pallas_call(
        functools.partial(kernel, D, CP, T, A, FEAT, EDGE, BLOCK, PIECE, scale),
        out_shape=(
            jax.ShapeDtypeStruct((BLOCK, D * CP), BF16),
            jax.ShapeDtypeStruct((A, FEAT), F32),
            jax.ShapeDtypeStruct((FEAT, FEAT), F32),
            jax.ShapeDtypeStruct((EDGE, FEAT), F32),
            jax.ShapeDtypeStruct((BLOCK, FEAT), F32),
        ),
        in_specs=[vmem] * 9,
        out_specs=(vmem,) * 5,
        scratch_shapes=[
            pltpu.VMEM((2 * W, FEAT + LANE), BF16),
            pltpu.VMEM((FULL, FEAT), BF16),
            pltpu.VMEM((D, FULL, CP), BF16),
            pltpu.VMEM((D, FULL, CP), BF16),
            pltpu.VMEM((D, FULL, CP), BF16),
            pltpu.VMEM((D, FULL, CP), BF16),
            pltpu.VMEM((8, T), F32),
            pltpu.VMEM((T, 8), F32),
            pltpu.VMEM((T, FEAT), BF16),
            pltpu.VMEM((T, FEAT), BF16),
            pltpu.VMEM((T, FEAT), BF16),
            pltpu.VMEM((T, FEAT), BF16),
            pltpu.VMEM((T, FEAT), F32),
            pltpu.VMEM((FULL, T), BF16),
            pltpu.VMEM((FULL, T), BF16),
            pltpu.VMEM((FULL, T), F32),
            pltpu.VMEM((2 * W, FEAT), F32),
            pltpu.VMEM((2 * W, FEAT), BF16),
            pltpu.VMEM((4, RIM, FEAT), BF16),
            pltpu.VMEM((A, FEAT), BF16),
            pltpu.VMEM((FULL, FEAT), F32),
            pltpu.VMEM((2 * R, LANE), F32),
            pltpu.VMEM((R, LANE), BF16),
            pltpu.VMEM((R, LANE), BF16),
            pltpu.VMEM((R, LANE), BF16),
            pltpu.VMEM((D, PIECE, LANE), BF16),
            pltpu.VMEM((2 * R, LANE), BF16),
            dma((5,)), dma((5,)), dma((D,)), dma((D,)), dma((D,)), dma((D,)), dma((5,)), dma((5,)),
            dma, dma, dma((D,)), dma((D,)), dma((D,)), dma((D,)), dma((D,)), dma((D,)),
        ],
        compiler_params=pltpu.CompilerParams(
            collective_id=0, has_side_effects=True, vmem_limit_bytes=56 * 1024 * 1024
        ),
        cost_estimate=pl.CostEstimate(flops=15 * 10**9, bytes_accessed=10**7, transcendentals=T * FEAT),
    )(features[0], orbitals, pair_list[0].T, owners[0].T, edge_feats[0], cot, w_pair, w_edge, w_block.T)
    blocks = outs[0]
    if CP != C:
        blocks = blocks.reshape(BLOCK, D, CP)[:, :, 0:C].reshape(BLOCK, S)
    return (blocks.T[None], outs[1][None], outs[2], outs[3], outs[4].T)


def solution(mesh):
    spread = P("slab", ("groups", "dom"), None)
    in_specs = (spread, P("slab", ("groups", "dom")), spread, spread, spread, spread, P(), P(), P())
    out_specs = (spread, spread, P("groups", None), P("groups", None), P("groups", None))
    return jax.shard_map(shards, mesh=mesh, in_specs=in_specs, out_specs=out_specs, check_vma=False)
```

```python
import functools

import jax
import jax.numpy as jnp
from jax import lax
from jax.experimental import pallas as pl
from jax.experimental.pallas import tpu as pltpu
from jax.sharding import PartitionSpec as P

ORB = 13
RIM = 32
LANE = 128
TILE = 256
F32 = jnp.float32
BF16 = jnp.bfloat16


def nn(a, b):
    return jnp.dot(a, b, preferred_element_type=F32)


def nt(a, b):
    return lax.dot_general(a, b, (((1,), (1,)), ((), ())), preferred_element_type=F32)


def tn(a, b):
    return lax.dot_general(a, b, (((0,), (0,)), ((), ())), preferred_element_type=F32)


def bits(cond):
    return jnp.where(cond, 1.0, 0.0).astype(BF16)


def iota(shape, dim):
    return lax.broadcasted_iota(jnp.int32, shape, dim)


def orbital_of(lanes):
    row = jnp.zeros_like(lanes)
    for k in range(1, 20):
        row = row + jnp.where(lanes >= ORB * k, 1, 0)
    return row.astype(F32), (lanes - ORB * row).astype(F32)


def kernel(
    D, C, T, A, FEAT, EDGE, BLOCK, PIECE, scale,
    feat_ref, orb_ref, pair_ref, own_ref, edge_in, cot_in, wp_in, we_ref, wb_ref,
    bo_ref, ag_ref, gp_ref, ge_ref, gb_ref,
    tab, wbp, cs, cr, bs, br, vr, vc, xo_s, xn_s, prod_s, act_s, ds_s, mask_s, blk, dc,
    gt, gtb, gr, grp, gba, g32, gas, gar, hs, rb, fin,
    cot_ref, edge_ref, wp_ref, load_s,
    halo_s, halo_r, cot_s, cot_r, blk_s, blk_r, grad_s, grad_r, sum_s, sum_r, red_s, red_r,
    all_s, all_r, fwd_s, fwd_r,
):
    W = A + 2 * RIM
    FULL = wbp.shape[0]
    CUT = FULL - 16
    R = D * PIECE
    me = lax.axis_index("dom")
    slab = lax.axis_index("slab")
    other = 1 - slab
    nxt = lax.rem(me + 1, D)
    prv = lax.rem(me + D - 1, D)
    ntile = T // TILE

    def rcopy(src, dst, ssem, rsem, dom, layer):
        return pltpu.make_async_remote_copy(
            src_ref=src, dst_ref=dst, send_sem=ssem, recv_sem=rsem,
            device_id={"dom": dom, "slab": layer}, device_id_type=pl.DeviceIdType.MESH,
        )

    def peer(k):
        i = k - 1
        return lax.rem(me + D // 2 + (1 - 2 * (i % 2)) * ((i + 1) // 2), D)

    def source(k):
        i = k - 1
        return lax.rem(me + 2 * D - D // 2 - (1 - 2 * (i % 2)) * ((i + 1) // 2), D)

    def rows_at(t):
        return pl.ds(pl.multiple_of(t * TILE, TILE), TILE)

    loads = [
        pltpu.make_async_copy(cot_in, cot_ref, load_s.at[0]),
        pltpu.make_async_copy(edge_in, edge_ref, load_s.at[1]),
        pltpu.make_async_copy(wp_in, wp_ref, load_s.at[2]),
    ]
    for load in loads:
        load.start()

    barrier = pltpu.get_barrier_semaphore()

    @pl.loop(1, D)
    def _(k):
        pl.semaphore_signal(barrier, inc=1, device_id={"dom": peer(k), "slab": slab}, device_id_type=pl.DeviceIdType.MESH)

    for dom in (me, nxt, prv):
        pl.semaphore_signal(barrier, inc=1, device_id={"dom": dom, "slab": other}, device_id_type=pl.DeviceIdType.MESH)

    diag = jnp.where(iota((A, A), 0) == iota((A, A), 1), orb_ref[...].astype(F32), 0.0).astype(BF16)
    tab[RIM:RIM + A, 0:FEAT] = feat_ref[...]
    tab[RIM:RIM + A, FEAT:FEAT + LANE] = nn(diag, jnp.ones((A, LANE), BF16)).astype(BF16)
    cs[:, CUT:FULL, :] = jnp.zeros((D, 16, C), BF16)
    cr[me, CUT:FULL, :] = jnp.zeros((16, C), BF16)

    def take_cot(d, dst):
        at = pl.ds(pl.multiple_of(d * C, C), C)
        dst[d, 0:CUT, :] = cot_ref[0:CUT, at]
        dst[d, CUT:BLOCK, :] = cot_ref[CUT:BLOCK, at]

    loads[0].wait()

    @pl.loop(1, D)
    def _(k):
        take_cot(peer(k), cs)

    take_cot(me, cr)
    pl.semaphore_wait(barrier, D + 2)

    head = tab.at[RIM:2 * RIM]
    tail = tab.at[A:A + RIM]
    halos = [
        rcopy(tail, tab.at[0:RIM], halo_s.at[0], halo_r.at[0], nxt, slab),
        rcopy(head, tab.at[RIM + A:W], halo_s.at[1], halo_r.at[1], prv, slab),
        rcopy(tail, tab.at[W:W + RIM], halo_s.at[2], halo_r.at[2], nxt, other),
        rcopy(head, tab.at[W + RIM + A:2 * W], halo_s.at[3], halo_r.at[3], prv, other),
        rcopy(tab.at[RIM:RIM + A], tab.at[W + RIM:W + RIM + A], halo_s.at[4], halo_r.at[4], me, other),
    ]
    for h in halos:
        h.start()

    def exchange(src, dst, ssem, rsem, d, at):
        return rcopy(src.at[d], dst.at[at], ssem.at[d], rsem.at[at], d, slab)

    @pl.loop(1, D)
    def _(k):
        exchange(cs, cr, cot_s, cot_r, peer(k), me).start()

    wbp[CUT:FULL, :] = jnp.zeros((16, FEAT), BF16)
    wbp[0:CUT, :] = wb_ref[0:CUT, :]
    wbp[CUT:BLOCK, :] = wb_ref[CUT:BLOCK, :]

    def table_row(raw):
        return jnp.where(raw >= 3 * A, raw - 3 * A + W, raw) - (A - RIM)

    DP = max(16, D)
    upper = bits(iota((TILE, TILE), 0) <= iota((TILE, TILE), 1))
    down = jnp.zeros((DP, 1), F32)
    vr[0:1, :] = pair_ref[0:1, :].astype(F32)
    vr[1:2, :] = table_row(pair_ref[1:2, :]).astype(F32)
    vr[3:8, :] = jnp.zeros((5, T), F32)
    for t in range(ntile):
        at = slice(t * TILE, (t + 1) * TILE)
        ow = own_ref[0:1, at]
        hit = jnp.where(iota((DP, TILE), 0) == ow, 1.0, 0.0)
        rank = nn(hit.astype(BF16), upper) + down
        slot = jnp.sum(hit * rank, axis=0, keepdims=True) - 1.0
        vr[2:3, at] = (ow * C).astype(F32) + slot
        down = down + jnp.sum(hit, axis=1, keepdims=True)
        vc[at, :] = vr[:, at].T

    for h in halos:
        h.wait_recv()
    loads[1].wait()
    loads[2].wait()

    entry = iota((FULL, 1), 0)
    div, mod = orbital_of(entry)
    first = bits(iota((16, LANE), 1) == 0)
    count_all = nt(first, tab[:, FEAT:FEAT + LANE]).astype(BF16)
    count_own = nt(first, tab[RIM:RIM + A, FEAT:FEAT + LANE]).astype(BF16)
    lanes_own = iota((TILE, A), 1).astype(F32)
    lanes_near = iota((TILE, 2 * W), 1).astype(F32)

    def hits_row(at):
        own = bits(iota((A, TILE), 0).astype(F32) == vr[0:1, at])
        near = bits(iota((2 * W, TILE), 0).astype(F32) == vr[1:2, at])
        return own, near

    @pl.loop(0, ntile)
    def _(t):
        at = rows_at(t)
        own_hit, near_hit = hits_row(at)
        no = nn(count_own, own_hit)[0:1, :]
        near = nn(count_all, near_hit)[0:1, :]
        keep = (div < no) & (mod < near)
        mask_s[:, at] = bits(keep)
        xo = nn(bits(lanes_own == vc[at, 0:1]), tab[RIM:RIM + A, 0:FEAT])
        xn = nn(bits(lanes_near == vc[at, 1:2]), tab[:, 0:FEAT])
        xo_s[at, :] = xo.astype(BF16)
        xn_s[at, :] = xn.astype(BF16)
        prod = (xo * xn).astype(BF16)
        prod_s[at, :] = prod
        pre = nn(prod, wp_ref[...]) + nn(edge_ref[at, :], we_ref[...])
        sg = jax.nn.sigmoid(pre)
        act = (pre * sg).astype(BF16)
        act_s[at, :] = act
        ds_s[at, :] = sg * (1.0 + pre * (1.0 - sg))
        blk[:, at] = jnp.where(keep, nt(wbp[...], act), 0.0).astype(BF16)

    STEP = 2 * TILE

    def pack_blocks(d, dst):
        acc = jnp.zeros((FULL, C), F32)
        base = (d * C).astype(F32)
        slot_of = iota((STEP, C), 1).astype(F32)
        for j in range(T // STEP):
            at = slice(j * STEP, (j + 1) * STEP)
            acc = acc + nn(blk[:, at], bits(slot_of == vc[at, 2:3] - base))
        dst[d] = acc.astype(BF16)

    @pl.loop(1, D)
    def _(k):
        d = peer(k)
        pack_blocks(d, bs)
        exchange(bs, br, blk_s, blk_r, d, me).start()

    pack_blocks(me, br)

    dc[...] = jnp.zeros_like(dc)

    def collect(d):
        base = (d * C).astype(F32)
        slot_of = iota((C, STEP), 0).astype(F32)
        for j in range(T // STEP):
            at = slice(j * STEP, (j + 1) * STEP)
            dc[:, at] += nn(cr[d], bits(slot_of == vr[2:3, at] - base))

    collect(me)

    @pl.loop(1, D)
    def _(k):
        d = source(k)
        exchange(cs, cr, cot_s, cot_r, d, d).wait_recv()
        collect(d)

    gt[...] = jnp.zeros_like(gt)
    gp_ref[...] = jnp.zeros_like(gp_ref)
    ge_ref[...] = jnp.zeros_like(ge_ref)
    gba[...] = jnp.zeros_like(gba)

    @pl.loop(0, ntile)
    def _(t):
        at = rows_at(t)
        dblock = (dc[:, at] * mask_s[:, at].astype(F32)).astype(BF16)
        dact = tn(dblock, wbp[...])
        dpre = (dact * ds_s[at, :]).astype(BF16)
        gp_ref[...] += tn(prod_s[at, :], dpre)
        ge_ref[...] += tn(edge_ref[at, :], dpre)
        gba[...] += nn(dblock, act_s[at, :])
        dprod = nt(dpre, wp_ref[...])
        to_own = (dprod * xn_s[at, :].astype(F32)).astype(BF16)
        to_near = (dprod * xo_s[at, :].astype(F32)).astype(BF16)
        own_hit, near_hit = hits_row(at)
        gt[...] += nn(near_hit, to_near)
        gt[RIM:RIM + A, :] += nn(own_hit, to_own)

    if 2 * R > 4 * (FEAT + EDGE + FULL):
        g32[4 * (FEAT + EDGE + FULL):2 * R, :] = jnp.zeros((2 * R - 4 * (FEAT + EDGE + FULL), LANE), F32)
    for c in range(4):
        g32[c * FEAT:(c + 1) * FEAT, :] = gp_ref[:, c * LANE:(c + 1) * LANE]
        g32[4 * FEAT + c * EDGE:4 * FEAT + (c + 1) * EDGE, :] = ge_ref[:, c * LANE:(c + 1) * LANE]
    low = 4 * FEAT + 4 * EDGE
    for c in range(4):
        g32[low + c * FULL:low + (c + 1) * FULL, :] = gba[:, c * LANE:(c + 1) * LANE]
    gas[...] = g32[pl.ds(pl.multiple_of(other * R, 16), R), :].astype(BF16)
    swap = rcopy(gas, gar, sum_s, sum_r, me, other)
    swap.start()

    gtb[...] = gt[...].astype(BF16)
    grads = [
        rcopy(gtb.at[0:RIM], gr.at[0], grad_s.at[0], grad_r.at[0], prv, slab),
        rcopy(gtb.at[RIM + A:W], gr.at[1], grad_s.at[1], grad_r.at[1], nxt, slab),
        rcopy(gtb.at[W:W + RIM], gr.at[2], grad_s.at[2], grad_r.at[2], prv, other),
        rcopy(gtb.at[W + RIM + A:2 * W], gr.at[3], grad_s.at[3], grad_r.at[3], nxt, other),
        rcopy(gtb.at[W + RIM:W + RIM + A], grp, grad_s.at[4], grad_r.at[4], me, other),
    ]
    for g in grads:
        g.start()

    swap.wait_recv()
    hs[...] = (g32[pl.ds(pl.multiple_of(slab * R, 16), R), :] + gar[...].astype(F32)).astype(BF16)

    def piece(d, of=0):
        return pl.ds(pl.multiple_of(of * R + d * PIECE, 16), PIECE)

    def reduce_copy(d, at):
        return rcopy(hs.at[piece(d)], rb.at[at], red_s.at[d], red_r.at[at], d, slab)

    @pl.loop(1, D)
    def _(k):
        reduce_copy(peer(k), me).start()

    for g in grads:
        g.wait_recv()
    ag_ref[...] = gt[RIM:RIM + A, :] + grp[...].astype(F32)
    ag_ref[A - RIM:A, :] += gr[0].astype(F32) + gr[2].astype(F32)
    ag_ref[0:RIM, :] += gr[1].astype(F32) + gr[3].astype(F32)

    def add_up(k, total):
        s = source(k)
        reduce_copy(s, s).wait_recv()
        return total + rb[s].astype(F32)

    total = lax.fori_loop(1, D, add_up, g32[piece(me, slab), :] + gar[piece(me), :].astype(F32))
    fin[piece(me, slab), :] = total.astype(BF16)

    def gather_copy(d, at):
        return rcopy(fin.at[piece(at, slab)], fin.at[piece(at, slab)], all_s.at[d], all_r.at[at], d, slab)

    def forward_copy(s, of):
        return rcopy(fin.at[piece(s, of)], fin.at[piece(s, of)], fwd_s.at[s], fwd_r.at[s], me, other)

    @pl.loop(1, D)
    def _(k):
        gather_copy(peer(k), me).start()

    forward_copy(me, slab).start()

    def unpack(d):
        at = pl.ds(pl.multiple_of(d * C, C), C)
        bo_ref[0:CUT, at] = br[d, 0:CUT, :]
        bo_ref[CUT:BLOCK, at] = br[d, CUT:BLOCK, :]

    unpack(me)

    @pl.loop(1, D)
    def _(k):
        d = source(k)
        exchange(bs, br, blk_s, blk_r, d, d).wait_recv()
        unpack(d)

    @pl.loop(1, D)
    def _(k):
        s = source(k)
        gather_copy(s, s).wait_recv()
        forward_copy(s, slab).start()

    @pl.loop(0, D)
    def _(s):
        forward_copy(s, other).wait_recv()

    for c in range(4):
        gp_ref[:, c * LANE:(c + 1) * LANE] = fin[c * FEAT:(c + 1) * FEAT, :].astype(F32) * scale
        ge_ref[:, c * LANE:(c + 1) * LANE] = fin[4 * FEAT + c * EDGE:4 * FEAT + (c + 1) * EDGE, :].astype(F32) * scale
    for c in range(4):
        gb_ref[:, c * LANE:(c + 1) * LANE] = fin[low + c * FULL:low + c * FULL + BLOCK, :].astype(F32) * scale

    for h in halos + grads + [swap]:
        h.wait_send()

    @pl.loop(1, D)
    def _(k):
        d = peer(k)
        exchange(cs, cr, cot_s, cot_r, d, me).wait_send()
        exchange(bs, br, blk_s, blk_r, d, me).wait_send()
        reduce_copy(d, me).wait_send()
        gather_copy(d, me).wait_send()

    @pl.loop(0, D)
    def _(s):
        forward_copy(s, slab).wait_send()


def shards(features, orbitals, pair_list, owners, edge_feats, cotangent, w_pair, w_edge, w_block):
    A, FEAT = features.shape[1:]
    T = pair_list.shape[1]
    D = lax.axis_size("dom")
    S, BLOCK = cotangent.shape[1:]
    EDGE = edge_feats.shape[2]
    C = S // D
    CP = -(-C // LANE) * LANE
    W = A + 2 * RIM
    FULL = -(-BLOCK // 16) * 16
    flat = 4 * (FEAT + EDGE + FULL)
    PIECE = -(-flat // (2 * D * 16)) * 16
    R = D * PIECE
    scale = float(lax.axis_size("slab") * D * T) ** (-0.5)
    cot = cotangent[0].T
    if CP != C:
        cot = jnp.pad(cot.reshape(BLOCK, D, C), ((0, 0), (0, 0), (0, CP - C))).reshape(BLOCK, D * CP)
    dma = pltpu.SemaphoreType.DMA
    vmem = pl.BlockSpec(memory_space=pltpu.VMEM)
    outs = pl.pallas_call(
        functools.partial(kernel, D, CP, T, A, FEAT, EDGE, BLOCK, PIECE, scale),
        out_shape=(
            jax.ShapeDtypeStruct((BLOCK, D * CP), BF16),
            jax.ShapeDtypeStruct((A, FEAT), F32),
            jax.ShapeDtypeStruct((FEAT, FEAT), F32),
            jax.ShapeDtypeStruct((EDGE, FEAT), F32),
            jax.ShapeDtypeStruct((BLOCK, FEAT), F32),
        ),
        in_specs=[vmem] * 4 + [pl.BlockSpec(memory_space=pl.ANY)] * 3 + [vmem] * 2,
        out_specs=(vmem,) * 5,
        scratch_shapes=[
            pltpu.VMEM((2 * W, FEAT + LANE), BF16),
            pltpu.VMEM((FULL, FEAT), BF16),
            pltpu.VMEM((D, FULL, CP), BF16),
            pltpu.VMEM((D, FULL, CP), BF16),
            pltpu.VMEM((D, FULL, CP), BF16),
            pltpu.VMEM((D, FULL, CP), BF16),
            pltpu.VMEM((8, T), F32),
            pltpu.VMEM((T, 8), F32),
            pltpu.VMEM((T, FEAT), BF16),
            pltpu.VMEM((T, FEAT), BF16),
            pltpu.VMEM((T, FEAT), BF16),
            pltpu.VMEM((T, FEAT), BF16),
            pltpu.VMEM((T, FEAT), F32),
            pltpu.VMEM((FULL, T), BF16),
            pltpu.VMEM((FULL, T), BF16),
            pltpu.VMEM((FULL, T), F32),
            pltpu.VMEM((2 * W, FEAT), F32),
            pltpu.VMEM((2 * W, FEAT), BF16),
            pltpu.VMEM((4, RIM, FEAT), BF16),
            pltpu.VMEM((A, FEAT), BF16),
            pltpu.VMEM((FULL, FEAT), F32),
            pltpu.VMEM((2 * R, LANE), F32),
            pltpu.VMEM((R, LANE), BF16),
            pltpu.VMEM((R, LANE), BF16),
            pltpu.VMEM((R, LANE), BF16),
            pltpu.VMEM((D, PIECE, LANE), BF16),
            pltpu.VMEM((2 * R, LANE), BF16),
            pltpu.VMEM((BLOCK, D * CP), BF16),
            pltpu.VMEM((T, EDGE), BF16),
            pltpu.VMEM((FEAT, FEAT), BF16),
            dma((3,)),
            dma((5,)), dma((5,)), dma((D,)), dma((D,)), dma((D,)), dma((D,)), dma((5,)), dma((5,)),
            dma, dma, dma((D,)), dma((D,)), dma((D,)), dma((D,)), dma((D,)), dma((D,)),
        ],
        compiler_params=pltpu.CompilerParams(
            collective_id=0, has_side_effects=True, vmem_limit_bytes=56 * 1024 * 1024
        ),
        cost_estimate=pl.CostEstimate(flops=15 * 10**9, bytes_accessed=10**7, transcendentals=T * FEAT),
    )(features[0], orbitals, pair_list[0].T, owners[0].T, edge_feats[0], cot, w_pair, w_edge, w_block.T)
    blocks = outs[0]
    if CP != C:
        blocks = blocks.reshape(BLOCK, D, CP)[:, :, 0:C].reshape(BLOCK, S)
    return (blocks.T[None], outs[1][None], outs[2], outs[3], outs[4].T)


def solution(mesh):
    spread = P("slab", ("groups", "dom"), None)
    in_specs = (spread, P("slab", ("groups", "dom")), spread, spread, spread, spread, P(), P(), P())
    out_specs = (spread, spread, P("groups", None), P("groups", None), P("groups", None))
    return jax.shard_map(shards, mesh=mesh, in_specs=in_specs, out_specs=out_specs, check_vma=False)
```
